512 devices in a mesh: grp: 16 (over z), blk: 32 (over y, x, core).
Axes of the slice: x: 4, y: 4, z: 16, core: 2. Of those that a mesh axis runs over, the one named last changes fastest.
Arguments:
- field: float32 [16, 256, 512, 256], P(None, 'blk', 'grp')
- start: float32 [256, 64], replicated, may hold values from -6 to 6
Outputs:
- core: float32 [16, 64, 512, 256], P('grp', 'blk')
- basis: float32 [256, 64], replicated
The draws below stay inside these ranges and needn't reach their ends.
All inputs are finite; a program needn't handle non-finite values.
Results may differ from the reference program's by a relative error of at most 0.0004.
Values sent between devices are 32-bit elements; how exact they have to be, the bound alone decides.
A program may use at most 64 MiB of HBM per device.

```python
import jax
import jax.numpy as jnp
from jax import lax

N1 = 256
VARS = 16
RANK = 64
ITERS = 3
N3 = 256
N2 = 512


def draw_field(key, part):
    key = jax.random.fold_in(key, 11)
    keys = jax.random.split(key, 6)
    noise = jax.random.normal(keys[0], (VARS, N1, N2, N3), jnp.float32)
    rise = 2.0
    scales = jnp.exp(jax.random.uniform(keys[1], (N1,), jnp.float32, -0.7, 0.7))
    mixing = jax.random.normal(keys[2], (N1, 4), jnp.float32) * 0.8
    var_mix = jax.random.normal(keys[3], (VARS, 4), jnp.float32)
    common = jax.random.normal(keys[4], (4, N2, N3), jnp.float32)
    total = scales[None, :, None, None] * noise
    for term in range(4):
        total = total + (mixing[:, term][None, :, None] * var_mix[:, term][:, None, None])[:, :, :, None] * common[term][None, None]
    ramp = 1.0 + rise * jnp.arange(N2, dtype=jnp.float32) / max(N2 - 1, 1)
    var_scale = jnp.exp(jax.random.uniform(keys[5], (VARS,), jnp.float32, -0.7, 0.7))
    return total * ramp[None, None, :, None] * var_scale[:, None, None, None]


def scatter_about(key, shape, spread, reach, held_as=jnp.bfloat16):
    return jnp.clip(spread * jax.random.normal(key, shape, jnp.float32), -reach, reach).astype(held_as)


def setup_inputs(seed: int = 0) -> dict:
    key_list = jax.random.split(jax.random.key(seed), 3)
    field = draw_field(jax.random.fold_in(key_list[2], 71), 0)
    start = scatter_about(key_list[1], (N1, RANK), 1.0, 6.0, jnp.float32)
    return dict(field=field, start=start)


def orth_once(block):
    small = jnp.dot(block.T, block, precision=lax.Precision.HIGHEST)
    lower = jnp.linalg.cholesky(small)
    return lax.linalg.triangular_solve(lower, block, left_side=False, lower=True, transpose_a=True)

def reference(field, start):
    count = field.shape[0] * field.shape[2] * field.shape[3]
    flat = field.reshape(field.shape[0], field.shape[1], -1)
    gram = jnp.einsum('vic,vjc->ij', flat, flat, precision=lax.Precision.HIGHEST) / count
    basis = start
    for step in range(ITERS):
        basis = orth_once(orth_once(jnp.dot(gram, basis, precision=lax.Precision.HIGHEST)))
    core = jnp.einsum('ir,vinm->vrnm', basis, field, precision=lax.Precision.HIGHEST)
    return (core, basis)
```

```python
import functools

import jax
import jax.numpy as jnp
from jax import lax
from jax.experimental import pallas as pl
from jax.experimental.pallas import tpu as pltpu
from jax.sharding import PartitionSpec as P

ITERS = 3
MESH = pl.DeviceIdType.MESH
HIGHEST = lax.Precision.HIGHEST
ANY = pl.BlockSpec(memory_space=pl.ANY)
VMEM = pl.BlockSpec(memory_space=pltpu.VMEM)
NX = 4
NC = 2
ZL = 4


def place(k):
    return k // (NX * NC), (k // NC) % NX, k % NC


def shifted(k, step, ny):
    y, x, core = place(k)
    dy, dx, dcore = place(step)
    return (((y + dy) % ny) * NX + (x + dx) % NX) * NC + (core + dcore) % NC


def wait_bytes(ref, sem):
    pltpu.make_async_copy(ref, ref, sem).wait()


def take(ref, c, a):
    parts, blocks, rows = ref.shape[:3]
    return ref.reshape(parts, blocks * rows, 128)[c, pl.ds(a, blocks, stride=rows), :]


def put(ref, c, a, value):
    parts, blocks, rows = ref.shape[:3]
    ref.reshape(parts, blocks * rows, 128)[c, pl.ds(a, blocks, stride=rows), :] = value


def inverse_factor(small, rank):
    lane = lax.broadcasted_iota(jnp.int32, (rank, 128), 1)
    row = lax.broadcasted_iota(jnp.int32, (rank, 128), 0)
    first = row[:8]
    tail = jnp.where(lane < 64, jnp.where(lane == row, 1.0, 0.0), small[:rank])
    done = []
    for b in range(rank // 8):
        below = row[: rank - 8 * b]
        columns = [
            jnp.broadcast_to(tail[:, 64 + 8 * b + s : 64 + 8 * b + s + 1], tail.shape) for s in range(8)
        ]
        pivots = jnp.ones((8, 128), jnp.float32)
        for t in range(8):
            pivot = columns[t][t : t + 1, :]
            pivots = jnp.where(first == t, pivot, pivots)
            factor = jnp.where(below > t, columns[t] * (1.0 / pivot), 0.0)
            for s in range(t + 1, 8):
                columns[s] = columns[s] - factor * columns[s][t : t + 1, :]
            tail = tail - factor * tail[t : t + 1, :]
        done.append(tail[:8] / jnp.sqrt(pivots))
        tail = tail[8:]
    return jnp.where(lane < rank, jnp.concatenate(done, axis=0), 0.0)


def split(value):
    high = value.astype(jnp.bfloat16)
    return high, (value - high.astype(jnp.float32)).astype(jnp.bfloat16)


def product(a, b, contract):
    return lax.dot_general(a, b, (contract, ((), ())), preferred_element_type=jnp.float32)


def exact(a, b, contract):
    return lax.dot_general(a, b, (contract, ((), ())), precision=HIGHEST, preferred_element_type=jnp.float32)


def kernel(
    nz,
    nk,
    count,
    field,
    start,
    out,
    basis_out,
    cols,
    core,
    part,
    cross,
    rows_in,
    mine,
    near_in,
    near_sum,
    far_in,
    total,
    held,
    cols_send,
    cols_recv,
    send_sem,
    recv_sem,
    core_send,
    core_recv,
):
    g, k = lax.axis_index("grp"), lax.axis_index("blk")
    ny = nk // (NX * NC)
    chunks, rank, na = core.shape[0], core.shape[1], core.shape[2]
    ni, nb = field.shape[1], field.shape[3] // 128
    each = rank // nk
    y, x, side = place(k)
    zl, zh = g % ZL, g // ZL
    nh = nz // ZL

    def near(step):
        return zh * ZL + (zl + step) % ZL

    def far(step):
        return ((zh + step) % nh) * ZL + zl

    def other(s):
        step = (s - 1 + side * (nk // 2)) % (nk - 1) + 1
        return shifted(k, (step * 13) % nk, ny)

    barrier = pltpu.get_barrier_semaphore()

    def greet(z, blk):
        pl.semaphore_signal(barrier, inc=1, device_id=(z, blk), device_id_type=MESH)

    @pl.loop(1, nk)
    def _(s):
        greet(g, other(s))

    @pl.loop(1, ZL)
    def _(s):
        greet(near(s), k)

    @pl.loop(1, nh)
    def _(s):
        greet(far(s), k)

    pl.semaphore_wait(barrier, nk - 1 + ZL - 1 + nh - 1)

    def variable(c, x, side):
        zero = (NX - x) // NX
        up = x + c * (nz // 2 - 2 * x)
        down = nz - up + zero * (1 - 2 * c) * (nz // 4) + zero * c * (nz // 2)
        return (g + up + side * (down - up)) % nz

    def piece(c, dest):
        y, x, side = place(dest)
        a, b = y // nb, y % nb
        return field.at[
            variable(c, x, side), :, pl.ds(pl.multiple_of(a * na, na), na), pl.ds(pl.multiple_of(b * 128, 128), 128)
        ]

    def slot(c):
        return cols.at[c, pl.ds(k * ni, ni)]

    @pl.loop(0, chunks)
    def _(c):
        pltpu.make_async_copy(piece(c, k), slot(c), cols_recv.at[c]).start()

        @pl.loop(1, nk)
        def _(s):
            dest = other(s)
            pltpu.make_async_remote_copy(
                src_ref=piece(c, dest),
                dst_ref=slot(c),
                send_sem=cols_send.at[c],
                recv_sem=cols_recv.at[c],
                device_id=(g, dest),
                device_id_type=MESH,
            ).start()

    part[...] = jnp.zeros_like(part)
    cross[...] = jnp.zeros_like(cross)

    @pl.loop(0, chunks)
    def _(c):
        wait_bytes(cols.at[c], cols_recv.at[c])

        @pl.loop(0, na // 2)
        def _(p):
            high, low = split(jnp.concatenate([take(cols, c, 2 * p), take(cols, c, 2 * p + 1)], axis=1))
            part[...] += product(high, high, ((1,), (1,))) + product(low, low, ((1,), (1,)))
            cross[...] += product(high, low, ((1,), (1,)))

    part[...] += cross[...] + cross[...].T

    own = pl.ds(pl.multiple_of(k * 8, 8), 8)
    rows_in[k] = part[own, :]

    @pl.loop(1, nk)
    def _(s):
        dest = other(s)
        pltpu.make_async_remote_copy(
            src_ref=part.at[pl.ds(pl.multiple_of(dest * 8, 8), 8)],
            dst_ref=rows_in.at[k],
            send_sem=send_sem.at[0],
            recv_sem=recv_sem.at[0],
            device_id=(g, dest),
            device_id_type=MESH,
        ).start()

    wait_bytes(rows_in.at[pl.ds(0, nk - 1)], recv_sem.at[0])
    mine[...] = jnp.sum(rows_in[...], axis=0)
    near_in[zl] = mine[...]

    @pl.loop(1, ZL)
    def _(s):
        pltpu.make_async_remote_copy(
            src_ref=mine,
            dst_ref=near_in.at[zl],
            send_sem=send_sem.at[1],
            recv_sem=recv_sem.at[1],
            device_id=(near(s), k),
            device_id_type=MESH,
        ).start()

    wait_bytes(near_in.at[pl.ds(0, ZL - 1)], recv_sem.at[1])
    near_sum[...] = jnp.sum(near_in[...], axis=0)
    far_in[zh] = near_sum[...]

    @pl.loop(1, nh)
    def _(s):
        pltpu.make_async_remote_copy(
            src_ref=near_sum,
            dst_ref=far_in.at[zh],
            send_sem=send_sem.at[2],
            recv_sem=recv_sem.at[2],
            device_id=(far(s), k),
            device_id_type=MESH,
        ).start()

    wait_bytes(far_in.at[pl.ds(0, nh - 1)], recv_sem.at[2])
    total[k] = jnp.sum(far_in[...], axis=0) * (1.0 / count)

    @pl.loop(1, nk)
    def _(s):
        pltpu.make_async_remote_copy(
            src_ref=total.at[k],
            dst_ref=total.at[k],
            send_sem=send_sem.at[3],
            recv_sem=recv_sem.at[3],
            device_id=(g, other(s)),
            device_id_type=MESH,
        ).start()

    wait_bytes(total.at[pl.ds(0, nk - 1)], recv_sem.at[3])

    half = start[...].T
    if rank < 64:
        half = jnp.concatenate([half, jnp.zeros((half.shape[0], 64 - rank), jnp.float32)], axis=1)
    held[...] = jnp.concatenate([half, half], axis=1)

    @pl.loop(0, ITERS)
    def _(step):
        held[...] = exact(total[...].reshape(part.shape), held[...], ((1,), (0,)))

        @pl.loop(0, 2)
        def _(again):
            block = held[...]
            factor = inverse_factor(exact(block, block, ((0,), (0,))), rank)
            if rank < 64:
                factor = jnp.concatenate([factor, jnp.zeros((64 - rank, 128), jnp.float32)], axis=0)
            held[...] = exact(block, jnp.concatenate([factor, factor], axis=0), ((1,), (1,)))

    turned = held[...].T[:rank]
    basis_out[...] = turned

    high, low = split(turned)
    both = jnp.concatenate([high, low], axis=0)
    place_out = out.at[
        0,
        :,
        pl.ds(pl.multiple_of((g * (ny // nb) + y // nb) * na, na), na),
        pl.ds(pl.multiple_of(y % nb * 128, 128), 128),
    ]

    @pl.loop(0, chunks)
    def _(c):
        v = variable(c, x, side)

        @pl.loop(0, na // 2)
        def _(p):
            block_high, block_low = split(
                jnp.concatenate([take(cols, c, 2 * p), take(cols, c, 2 * p + 1)], axis=1)
            )
            first = product(both, block_high, ((1,), (0,)))
            result = first[:rank] + (first[rank:] + product(high, block_low, ((1,), (0,))))
            for h in range(2):
                put(core, c, 2 * p + h, result[:, 128 * h : 128 * h + 128])

        def send(dest):
            pltpu.make_async_remote_copy(
                src_ref=core.at[c, pl.ds(dest * each, each)],
                dst_ref=place_out,
                send_sem=core_send,
                recv_sem=core_recv,
                device_id=(v, dest),
                device_id_type=MESH,
            ).start()

        @pl.loop(1, nk)
        def _(s):
            send(other(s))

        @pl.when(v == g)
        def _():
            pltpu.make_async_copy(core.at[c, pl.ds(k * each, each)], place_out, core_recv).start()

        @pl.when(v != g)
        def _():
            send(k)

    @pl.loop(0, chunks)
    def _(c):
        wait_bytes(cols.at[c, pl.ds(0, (nk - 1) * ni)], cols_send.at[c])

    wait_bytes(rows_in.at[pl.ds(0, nk - 1)], send_sem.at[0])
    wait_bytes(near_in.at[pl.ds(0, ZL - 1)], send_sem.at[1])
    wait_bytes(far_in.at[pl.ds(0, nh - 1)], send_sem.at[2])
    wait_bytes(total.at[pl.ds(0, nk - 1)], send_sem.at[3])

    wait_bytes(out, core_recv)

    @pl.when(x + side == 0)
    def _():
        wait_bytes(core.at[pl.ds(0, chunks - 1)], core_send)
        wait_bytes(core.at[chunks - 1, pl.ds(0, rank - each)], core_send)

    @pl.when(x + side != 0)
    def _():
        wait_bytes(core, core_send)


def local(nz, nk, field, start):
    nv, ni, na, nb = field.shape
    n1, rank = start.shape
    chunks = 2
    rows = na * nb * nv // (128 * nk * chunks)
    f32 = jnp.float32
    core, basis = pl.pallas_call(
        functools.partial(kernel, nz, nk, nv * na * nz * nb),
        out_shape=(
            jax.ShapeDtypeStruct((nv // nz, rank // nk, na * nz, nb), f32),
            jax.ShapeDtypeStruct((rank, n1), f32),
        ),
        in_specs=[ANY, VMEM],
        out_specs=(ANY, VMEM),
        scratch_shapes=[
            pltpu.VMEM((chunks, n1, rows, 128), f32),
            pltpu.VMEM((chunks, rank, rows, 128), f32),
            pltpu.VMEM((n1, n1), f32),
            pltpu.VMEM((n1, n1), f32),
            pltpu.VMEM((nk, 8, n1), f32),
            pltpu.VMEM((8, n1), f32),
            pltpu.VMEM((ZL, 8, n1), f32),
            pltpu.VMEM((8, n1), f32),
            pltpu.VMEM((nz // ZL, 8, n1), f32),
            pltpu.VMEM((nk, 8, n1), f32),
            pltpu.VMEM((n1, 128), f32),
            pltpu.SemaphoreType.DMA((chunks,)),
            pltpu.SemaphoreType.DMA((chunks,)),
            pltpu.SemaphoreType.DMA((4,)),
            pltpu.SemaphoreType.DMA((4,)),
            pltpu.SemaphoreType.DMA,
            pltpu.SemaphoreType.DMA,
        ],
        compiler_params=pltpu.CompilerParams(
            collective_id=0, has_side_effects=True, vmem_limit_bytes=60 * 2**20
        ),
        name="whole_step",
    )(field, start.T)
    return (core, basis.T)


def solution(mesh):
    placed = (P(None, "blk", "grp", None), P())
    return jax.shard_map(
        functools.partial(local, mesh.shape["grp"], mesh.shape["blk"]),
        mesh=mesh,
        in_specs=placed,
        out_specs=(P("grp", "blk", None, None), P()),
        check_vma=False,
    )
```

```python
import functools

import jax
import jax.numpy as jnp
from jax import lax
from jax.experimental import pallas as pl
from jax.experimental.pallas import tpu as pltpu
from jax.sharding import PartitionSpec as P

ITERS = 3
MESH = pl.DeviceIdType.MESH
HIGHEST = lax.Precision.HIGHEST
ANY = pl.BlockSpec(memory_space=pl.ANY)
VMEM = pl.BlockSpec(memory_space=pltpu.VMEM)
NX = 4
NC = 2
ZL = 4


def place(k):
    return k // (NX * NC), (k // NC) % NX, k % NC


def shifted(k, step, ny):
    y, x, core = place(k)
    dy, dx, dcore = place(step)
    return (((y + dy) % ny) * NX + (x + dx) % NX) * NC + (core + dcore) % NC


def wait_bytes(ref, sem):
    pltpu.make_async_copy(ref, ref, sem).wait()


def take(ref, c, a):
    parts, blocks, rows = ref.shape[:3]
    return ref.reshape(parts, blocks * rows, 128)[c, pl.ds(a, blocks, stride=rows), :]


def put(ref, c, a, value):
    parts, blocks, rows = ref.shape[:3]
    ref.reshape(parts, blocks * rows, 128)[c, pl.ds(a, blocks, stride=rows), :] = value


def inverse_factor(small, rank):
    lane = lax.broadcasted_iota(jnp.int32, (rank, 128), 1)
    row = lax.broadcasted_iota(jnp.int32, (rank, 128), 0)
    first = row[:8]
    tail = jnp.where(lane < 64, jnp.where(lane == row, 1.0, 0.0), small[:rank])
    done = []
    for b in range(rank // 8):
        below = row[: rank - 8 * b]
        columns = [
            jnp.broadcast_to(tail[:, 64 + 8 * b + s : 64 + 8 * b + s + 1], tail.shape) for s in range(8)
        ]
        pivots = jnp.ones((8, 128), jnp.float32)
        for t in range(8):
            pivot = columns[t][t : t + 1, :]
            pivots = jnp.where(first == t, pivot, pivots)
            factor = jnp.where(below > t, columns[t] * (1.0 / pivot), 0.0)
            for s in range(t + 1, 8):
                columns[s] = columns[s] - factor * columns[s][t : t + 1, :]
            tail = tail - factor * tail[t : t + 1, :]
        done.append(tail[:8] / jnp.sqrt(pivots))
        tail = tail[8:]
    return jnp.where(lane < rank, jnp.concatenate(done, axis=0), 0.0)


def split(value):
    high = value.astype(jnp.bfloat16)
    return high, (value - high.astype(jnp.float32)).astype(jnp.bfloat16)


def product(a, b, contract):
    return lax.dot_general(a, b, (contract, ((), ())), preferred_element_type=jnp.float32)


def exact(a, b, contract):
    return lax.dot_general(a, b, (contract, ((), ())), precision=HIGHEST, preferred_element_type=jnp.float32)


def kernel(
    nz,
    nk,
    count,
    field,
    start,
    out,
    basis_out,
    cols,
    core,
    part,
    cross,
    rows_in,
    mine,
    near_in,
    near_sum,
    far_in,
    total,
    held,
    cols_send,
    cols_recv,
    send_sem,
    recv_sem,
    core_send,
    core_recv,
):
    g, k = lax.axis_index("grp"), lax.axis_index("blk")
    ny = nk // (NX * NC)
    chunks, rank, na = core.shape[0], core.shape[1], core.shape[2]
    ni, nb = field.shape[1], field.shape[3] // 128
    each = rank // nk
    y, x, side = place(k)
    zl, zh = g % ZL, g // ZL
    nh = nz // ZL

    def near(step):
        return zh * ZL + (zl + step) % ZL

    def far(step):
        return ((zh + step) % nh) * ZL + zl

    def other(s):
        step = (s - 1 + side * (nk // 2)) % (nk - 1) + 1
        return shifted(k, (step * 13) % nk, ny)

    barrier = pltpu.get_barrier_semaphore()

    def greet(z, blk):
        pl.semaphore_signal(barrier, inc=1, device_id=(z, blk), device_id_type=MESH)

    @pl.loop(1, nk)
    def _(s):
        greet(g, other(s))

    @pl.loop(1, ZL)
    def _(s):
        greet(near(s), k)

    @pl.loop(1, nh)
    def _(s):
        greet(far(s), k)

    pl.semaphore_wait(barrier, nk - 1 + ZL - 1 + nh - 1)

    def variable(c, x, side):
        up = 1 + x + c * (nz // 2 - 1 - 2 * x)
        return (g + nz + up + side * (1 - 2 * up)) % nz

    def piece(c, dest):
        y, x, side = place(dest)
        a, b = y // nb, y % nb
        return field.at[
            variable(c, x, side), :, pl.ds(pl.multiple_of(a * na, na), na), pl.ds(pl.multiple_of(b * 128, 128), 128)
        ]

    def slot(c):
        return cols.at[c, pl.ds(k * ni, ni)]

    @pl.loop(0, chunks)
    def _(c):
        pltpu.make_async_copy(piece(c, k), slot(c), cols_recv.at[c]).start()

        @pl.loop(1, nk)
        def _(s):
            dest = other(s)
            pltpu.make_async_remote_copy(
                src_ref=piece(c, dest),
                dst_ref=slot(c),
                send_sem=cols_send.at[c],
                recv_sem=cols_recv.at[c],
                device_id=(g, dest),
                device_id_type=MESH,
            ).start()

    part[...] = jnp.zeros_like(part)
    cross[...] = jnp.zeros_like(cross)

    @pl.loop(0, chunks)
    def _(c):
        wait_bytes(cols.at[c], cols_recv.at[c])

        @pl.loop(0, na // 2)
        def _(p):
            high, low = split(jnp.concatenate([take(cols, c, 2 * p), take(cols, c, 2 * p + 1)], axis=1))
            part[...] += product(high, high, ((1,), (1,))) + product(low, low, ((1,), (1,)))
            cross[...] += product(high, low, ((1,), (1,)))

    part[...] += cross[...] + cross[...].T

    own = pl.ds(pl.multiple_of(k * 8, 8), 8)
    rows_in[k] = part[own, :]

    @pl.loop(1, nk)
    def _(s):
        dest = other(s)
        pltpu.make_async_remote_copy(
            src_ref=part.at[pl.ds(pl.multiple_of(dest * 8, 8), 8)],
            dst_ref=rows_in.at[k],
            send_sem=send_sem.at[0],
            recv_sem=recv_sem.at[0],
            device_id=(g, dest),
            device_id_type=MESH,
        ).start()

    wait_bytes(rows_in.at[pl.ds(0, nk - 1)], recv_sem.at[0])
    mine[...] = jnp.sum(rows_in[...], axis=0)
    near_in[zl] = mine[...]

    @pl.loop(1, ZL)
    def _(s):
        pltpu.make_async_remote_copy(
            src_ref=mine,
            dst_ref=near_in.at[zl],
            send_sem=send_sem.at[1],
            recv_sem=recv_sem.at[1],
            device_id=(near(s), k),
            device_id_type=MESH,
        ).start()

    wait_bytes(near_in.at[pl.ds(0, ZL - 1)], recv_sem.at[1])
    near_sum[...] = jnp.sum(near_in[...], axis=0)
    far_in[zh] = near_sum[...]

    @pl.loop(1, nh)
    def _(s):
        pltpu.make_async_remote_copy(
            src_ref=near_sum,
            dst_ref=far_in.at[zh],
            send_sem=send_sem.at[2],
            recv_sem=recv_sem.at[2],
            device_id=(far(s), k),
            device_id_type=MESH,
        ).start()

    wait_bytes(far_in.at[pl.ds(0, nh - 1)], recv_sem.at[2])
    total[k] = jnp.sum(far_in[...], axis=0) * (1.0 / count)

    @pl.loop(1, nk)
    def _(s):
        pltpu.make_async_remote_copy(
            src_ref=total.at[k],
            dst_ref=total.at[k],
            send_sem=send_sem.at[3],
            recv_sem=recv_sem.at[3],
            device_id=(g, other(s)),
            device_id_type=MESH,
        ).start()

    wait_bytes(total.at[pl.ds(0, nk - 1)], recv_sem.at[3])

    half = start[...].T
    if rank < 64:
        half = jnp.concatenate([half, jnp.zeros((half.shape[0], 64 - rank), jnp.float32)], axis=1)
    held[...] = jnp.concatenate([half, half], axis=1)

    @pl.loop(0, ITERS)
    def _(step):
        held[...] = exact(total[...].reshape(part.shape), held[...], ((1,), (0,)))

        @pl.loop(0, 2)
        def _(again):
            block = held[...]
            factor = inverse_factor(exact(block, block, ((0,), (0,))), rank)
            if rank < 64:
                factor = jnp.concatenate([factor, jnp.zeros((64 - rank, 128), jnp.float32)], axis=0)
            held[...] = exact(block, jnp.concatenate([factor, factor], axis=0), ((1,), (1,)))

    turned = held[...].T[:rank]
    basis_out[...] = turned

    high, low = split(turned)
    both = jnp.concatenate([high, low], axis=0)
    place_out = out.at[
        0,
        :,
        pl.ds(pl.multiple_of((g * (ny // nb) + y // nb) * na, na), na),
        pl.ds(pl.multiple_of(y % nb * 128, 128), 128),
    ]

    @pl.loop(0, chunks)
    def _(c):
        v = variable(c, x, side)

        @pl.loop(0, na // 2)
        def _(p):
            block_high, block_low = split(
                jnp.concatenate([take(cols, c, 2 * p), take(cols, c, 2 * p + 1)], axis=1)
            )
            first = product(both, block_high, ((1,), (0,)))
            result = first[:rank] + (first[rank:] + product(high, block_low, ((1,), (0,))))
            for h in range(2):
                put(core, c, 2 * p + h, result[:, 128 * h : 128 * h + 128])

        def send(dest):
            pltpu.make_async_remote_copy(
                src_ref=core.at[c, pl.ds(dest * each, each)],
                dst_ref=place_out,
                send_sem=core_send,
                recv_sem=core_recv,
                device_id=(v, dest),
                device_id_type=MESH,
            ).start()

        @pl.loop(1, nk)
        def _(s):
            send(other(s))

        @pl.when(v == g)
        def _():
            pltpu.make_async_copy(core.at[c, pl.ds(k * each, each)], place_out, core_recv).start()

        @pl.when(v != g)
        def _():
            send(k)

    @pl.loop(0, chunks)
    def _(c):
        wait_bytes(cols.at[c, pl.ds(0, (nk - 1) * ni)], cols_send.at[c])

    wait_bytes(rows_in.at[pl.ds(0, nk - 1)], send_sem.at[0])
    wait_bytes(near_in.at[pl.ds(0, ZL - 1)], send_sem.at[1])
    wait_bytes(far_in.at[pl.ds(0, nh - 1)], send_sem.at[2])
    wait_bytes(total.at[pl.ds(0, nk - 1)], send_sem.at[3])

    wait_bytes(out, core_recv)

    @pl.when(x + 1 - side == 0)
    def _():
        wait_bytes(core.at[pl.ds(0, chunks - 1)], core_send)
        wait_bytes(core.at[chunks - 1, pl.ds(0, rank - each)], core_send)

    @pl.when(x + 1 - side != 0)
    def _():
        wait_bytes(core, core_send)


def local(nz, nk, field, start):
    nv, ni, na, nb = field.shape
    n1, rank = start.shape
    chunks = 2
    rows = na * nb * nv // (128 * nk * chunks)
    f32 = jnp.float32
    core, basis = pl.pallas_call(
        functools.partial(kernel, nz, nk, nv * na * nz * nb),
        out_shape=(
            jax.ShapeDtypeStruct((nv // nz, rank // nk, na * nz, nb), f32),
            jax.ShapeDtypeStruct((rank, n1), f32),
        ),
        in_specs=[ANY, VMEM],
        out_specs=(ANY, VMEM),
        scratch_shapes=[
            pltpu.VMEM((chunks, n1, rows, 128), f32),
            pltpu.VMEM((chunks, rank, rows, 128), f32),
            pltpu.VMEM((n1, n1), f32),
            pltpu.VMEM((n1, n1), f32),
            pltpu.VMEM((nk, 8, n1), f32),
            pltpu.VMEM((8, n1), f32),
            pltpu.VMEM((ZL, 8, n1), f32),
            pltpu.VMEM((8, n1), f32),
            pltpu.VMEM((nz // ZL, 8, n1), f32),
            pltpu.VMEM((nk, 8, n1), f32),
            pltpu.VMEM((n1, 128), f32),
            pltpu.SemaphoreType.DMA((chunks,)),
            pltpu.SemaphoreType.DMA((chunks,)),
            pltpu.SemaphoreType.DMA((4,)),
            pltpu.SemaphoreType.DMA((4,)),
            pltpu.SemaphoreType.DMA,
            pltpu.SemaphoreType.DMA,
        ],
        compiler_params=pltpu.CompilerParams(
            collective_id=0, has_side_effects=True, vmem_limit_bytes=60 * 2**20
        ),
        name="whole_step",
    )(field, start.T)
    return (core, basis.T)


def solution(mesh):
    placed = (P(None, "blk", "grp", None), P())
    return jax.shard_map(
        functools.partial(local, mesh.shape["grp"], mesh.shape["blk"]),
        mesh=mesh,
        in_specs=placed,
        out_specs=(P("grp", "blk", None, None), P()),
        check_vma=False,
    )
```

```python
import functools

import jax
import jax.numpy as jnp
from jax import lax
from jax.experimental import pallas as pl
from jax.experimental.pallas import tpu as pltpu
from jax.sharding import PartitionSpec as P

ITERS = 3
MESH = pl.DeviceIdType.MESH
HIGHEST = lax.Precision.HIGHEST
ANY = pl.BlockSpec(memory_space=pl.ANY)
VMEM = pl.BlockSpec(memory_space=pltpu.VMEM)
NX = 4
NC = 2
ZL = 4


def place(k):
    return k // (NX * NC), (k // NC) % NX, k % NC


def shifted(k, step, ny):
    y, x, core = place(k)
    dy, dx, dcore = place(step)
    return (((y + dy) % ny) * NX + (x + dx) % NX) * NC + (core + dcore) % NC


def wait_bytes(ref, sem):
    pltpu.make_async_copy(ref, ref, sem).wait()


def take(ref, c, a):
    parts, blocks, rows = ref.shape[:3]
    return ref.reshape(parts, blocks * rows, 128)[c, pl.ds(a, blocks, stride=rows), :]


def put(ref, c, a, value):
    parts, blocks, rows = ref.shape[:3]
    ref.reshape(parts, blocks * rows, 128)[c, pl.ds(a, blocks, stride=rows), :] = value


def inverse_factor(small, rank):
    lane = lax.broadcasted_iota(jnp.int32, (rank, 128), 1)
    row = lax.broadcasted_iota(jnp.int32, (rank, 128), 0)
    first = row[:8]
    tail = jnp.where(lane < 64, jnp.where(lane == row, 1.0, 0.0), small[:rank])
    done = []
    for b in range(rank // 8):
        below = row[: rank - 8 * b]
        columns = [
            jnp.broadcast_to(tail[:, 64 + 8 * b + s : 64 + 8 * b + s + 1], tail.shape) for s in range(8)
        ]
        pivots = jnp.ones((8, 128), jnp.float32)
        for t in range(8):
            pivot = columns[t][t : t + 1, :]
            pivots = jnp.where(first == t, pivot, pivots)
            factor = jnp.where(below > t, columns[t] * (1.0 / pivot), 0.0)
            for s in range(t + 1, 8):
                columns[s] = columns[s] - factor * columns[s][t : t + 1, :]
            tail = tail - factor * tail[t : t + 1, :]
        done.append(tail[:8] / jnp.sqrt(pivots))
        tail = tail[8:]
    return jnp.where(lane < rank, jnp.concatenate(done, axis=0), 0.0)


def split(value):
    high = value.astype(jnp.bfloat16)
    return high, (value - high.astype(jnp.float32)).astype(jnp.bfloat16)


def product(a, b, contract):
    return lax.dot_general(a, b, (contract, ((), ())), preferred_element_type=jnp.float32)


def exact(a, b, contract):
    return lax.dot_general(a, b, (contract, ((), ())), precision=HIGHEST, preferred_element_type=jnp.float32)


def kernel(
    nz,
    nk,
    count,
    field,
    start,
    out,
    basis_out,
    cols,
    core,
    part,
    cross,
    rows_in,
    mine,
    near_in,
    near_sum,
    far_in,
    total,
    held,
    cols_send,
    cols_recv,
    send_sem,
    recv_sem,
    core_send,
    core_recv,
):
    g, k = lax.axis_index("grp"), lax.axis_index("blk")
    ny = nk // (NX * NC)
    chunks, rank, na = core.shape[0], core.shape[1], core.shape[2]
    ni, nb = field.shape[1], field.shape[3] // 128
    each = rank // nk
    y, x, side = place(k)
    zl, zh = g % ZL, g // ZL
    nh = nz // ZL

    def near(step):
        return zh * ZL + (zl + step) % ZL

    def far(step):
        return ((zh + step) % nh) * ZL + zl

    def other(s):
        step = (s - 1 + side * (nk // 2)) % (nk - 1) + 1
        return shifted(k, (step * 13) % nk, ny)

    barrier = pltpu.get_barrier_semaphore()

    def greet(z, blk):
        pl.semaphore_signal(barrier, inc=1, device_id=(z, blk), device_id_type=MESH)

    @pl.loop(1, nk)
    def _(s):
        greet(g, other(s))

    @pl.loop(1, ZL)
    def _(s):
        greet(near(s), k)

    @pl.loop(1, nh)
    def _(s):
        greet(far(s), k)

    pl.semaphore_wait(barrier, nk - 1 + ZL - 1 + nh - 1)

    def variable(c, x, side):
        up = 1 + x + c * (nz // 2 - 1 - 2 * x)
        return (g + nz + up - 2 * side * up + side * c * ((NX - x) // NX) * (nz // 2)) % nz

    def piece(c, dest):
        y, x, side = place(dest)
        a, b = y // nb, y % nb
        return field.at[
            variable(c, x, side), :, pl.ds(pl.multiple_of(a * na, na), na), pl.ds(pl.multiple_of(b * 128, 128), 128)
        ]

    def slot(c):
        return cols.at[c, pl.ds(k * ni, ni)]

    @pl.loop(0, chunks)
    def _(c):
        pltpu.make_async_copy(piece(c, k), slot(c), cols_recv.at[c]).start()

        @pl.loop(1, nk)
        def _(s):
            dest = other(s)
            pltpu.make_async_remote_copy(
                src_ref=piece(c, dest),
                dst_ref=slot(c),
                send_sem=cols_send.at[c],
                recv_sem=cols_recv.at[c],
                device_id=(g, dest),
                device_id_type=MESH,
            ).start()

    part[...] = jnp.zeros_like(part)
    cross[...] = jnp.zeros_like(cross)

    @pl.loop(0, chunks)
    def _(c):
        wait_bytes(cols.at[c], cols_recv.at[c])

        @pl.loop(0, na // 2)
        def _(p):
            high, low = split(jnp.concatenate([take(cols, c, 2 * p), take(cols, c, 2 * p + 1)], axis=1))
            part[...] += product(high, high, ((1,), (1,))) + product(low, low, ((1,), (1,)))
            cross[...] += product(high, low, ((1,), (1,)))

    part[...] += cross[...] + cross[...].T

    own = pl.ds(pl.multiple_of(k * 8, 8), 8)
    rows_in[k] = part[own, :]

    @pl.loop(1, nk)
    def _(s):
        dest = other(s)
        pltpu.make_async_remote_copy(
            src_ref=part.at[pl.ds(pl.multiple_of(dest * 8, 8), 8)],
            dst_ref=rows_in.at[k],
            send_sem=send_sem.at[0],
            recv_sem=recv_sem.at[0],
            device_id=(g, dest),
            device_id_type=MESH,
        ).start()

    wait_bytes(rows_in.at[pl.ds(0, nk - 1)], recv_sem.at[0])
    mine[...] = jnp.sum(rows_in[...], axis=0)
    near_in[zl] = mine[...]

    @pl.loop(1, ZL)
    def _(s):
        pltpu.make_async_remote_copy(
            src_ref=mine,
            dst_ref=near_in.at[zl],
            send_sem=send_sem.at[1],
            recv_sem=recv_sem.at[1],
            device_id=(near(s), k),
            device_id_type=MESH,
        ).start()

    wait_bytes(near_in.at[pl.ds(0, ZL - 1)], recv_sem.at[1])
    near_sum[...] = jnp.sum(near_in[...], axis=0)
    far_in[zh] = near_sum[...]

    @pl.loop(1, nh)
    def _(s):
        pltpu.make_async_remote_copy(
            src_ref=near_sum,
            dst_ref=far_in.at[zh],
            send_sem=send_sem.at[2],
            recv_sem=recv_sem.at[2],
            device_id=(far(s), k),
            device_id_type=MESH,
        ).start()

    wait_bytes(far_in.at[pl.ds(0, nh - 1)], recv_sem.at[2])
    total[k] = jnp.sum(far_in[...], axis=0) * (1.0 / count)

    @pl.loop(1, nk)
    def _(s):
        pltpu.make_async_remote_copy(
            src_ref=total.at[k],
            dst_ref=total.at[k],
            send_sem=send_sem.at[3],
            recv_sem=recv_sem.at[3],
            device_id=(g, other(s)),
            device_id_type=MESH,
        ).start()

    wait_bytes(total.at[pl.ds(0, nk - 1)], recv_sem.at[3])

    half = start[...].T
    if rank < 64:
        half = jnp.concatenate([half, jnp.zeros((half.shape[0], 64 - rank), jnp.float32)], axis=1)
    held[...] = jnp.concatenate([half, half], axis=1)

    @pl.loop(0, ITERS)
    def _(step):
        held[...] = exact(total[...].reshape(part.shape), held[...], ((1,), (0,)))

        @pl.loop(0, 2)
        def _(again):
            block = held[...]
            factor = inverse_factor(exact(block, block, ((0,), (0,))), rank)
            if rank < 64:
                factor = jnp.concatenate([factor, jnp.zeros((64 - rank, 128), jnp.float32)], axis=0)
            held[...] = exact(block, jnp.concatenate([factor, factor], axis=0), ((1,), (1,)))

    turned = held[...].T[:rank]
    basis_out[...] = turned

    high, low = split(turned)
    both = jnp.concatenate([high, low], axis=0)
    place_out = out.at[
        0,
        :,
        pl.ds(pl.multiple_of((g * (ny // nb) + y // nb) * na, na), na),
        pl.ds(pl.multiple_of(y % nb * 128, 128), 128),
    ]

    @pl.loop(0, chunks)
    def _(c):
        v = variable(c, x, side)

        @pl.loop(0, na // 2)
        def _(p):
            block_high, block_low = split(
                jnp.concatenate([take(cols, c, 2 * p), take(cols, c, 2 * p + 1)], axis=1)
            )
            first = product(both, block_high, ((1,), (0,)))
            result = first[:rank] + (first[rank:] + product(high, block_low, ((1,), (0,))))
            for h in range(2):
                put(core, c, 2 * p + h, result[:, 128 * h : 128 * h + 128])

        def send(dest):
            pltpu.make_async_remote_copy(
                src_ref=core.at[c, pl.ds(dest * each, each)],
                dst_ref=place_out,
                send_sem=core_send,
                recv_sem=core_recv,
                device_id=(v, dest),
                device_id_type=MESH,
            ).start()

        @pl.loop(1, nk)
        def _(s):
            send(other(s))

        @pl.when(v == g)
        def _():
            pltpu.make_async_copy(core.at[c, pl.ds(k * each, each)], place_out, core_recv).start()

        @pl.when(v != g)
        def _():
            send(k)

    @pl.loop(0, chunks)
    def _(c):
        wait_bytes(cols.at[c, pl.ds(0, (nk - 1) * ni)], cols_send.at[c])

    wait_bytes(rows_in.at[pl.ds(0, nk - 1)], send_sem.at[0])
    wait_bytes(near_in.at[pl.ds(0, ZL - 1)], send_sem.at[1])
    wait_bytes(far_in.at[pl.ds(0, nh - 1)], send_sem.at[2])
    wait_bytes(total.at[pl.ds(0, nk - 1)], send_sem.at[3])

    wait_bytes(out, core_recv)

    @pl.when(x + NC - 1 - side == 0)
    def _():
        wait_bytes(core.at[pl.ds(0, chunks - 1)], core_send)
        wait_bytes(core.at[chunks - 1, pl.ds(0, rank - each)], core_send)

    @pl.when(x + NC - 1 - side != 0)
    def _():
        wait_bytes(core, core_send)


def local(nz, nk, field, start):
    nv, ni, na, nb = field.shape
    n1, rank = start.shape
    chunks = 2
    rows = na * nb * nv // (128 * nk * chunks)
    f32 = jnp.float32
    core, basis = pl.pallas_call(
        functools.partial(kernel, nz, nk, nv * na * nz * nb),
        out_shape=(
            jax.ShapeDtypeStruct((nv // nz, rank // nk, na * nz, nb), f32),
            jax.ShapeDtypeStruct((rank, n1), f32),
        ),
        in_specs=[ANY, VMEM],
        out_specs=(ANY, VMEM),
        scratch_shapes=[
            pltpu.VMEM((chunks, n1, rows, 128), f32),
            pltpu.VMEM((chunks, rank, rows, 128), f32),
            pltpu.VMEM((n1, n1), f32),
            pltpu.VMEM((n1, n1), f32),
            pltpu.VMEM((nk, 8, n1), f32),
            pltpu.VMEM((8, n1), f32),
            pltpu.VMEM((ZL, 8, n1), f32),
            pltpu.VMEM((8, n1), f32),
            pltpu.VMEM((nz // ZL, 8, n1), f32),
            pltpu.VMEM((nk, 8, n1), f32),
            pltpu.VMEM((n1, 128), f32),
            pltpu.SemaphoreType.DMA((chunks,)),
            pltpu.SemaphoreType.DMA((chunks,)),
            pltpu.SemaphoreType.DMA((4,)),
            pltpu.SemaphoreType.DMA((4,)),
            pltpu.SemaphoreType.DMA,
            pltpu.SemaphoreType.DMA,
        ],
        compiler_params=pltpu.CompilerParams(
            collective_id=0, has_side_effects=True, vmem_limit_bytes=60 * 2**20
        ),
        name="whole_step",
    )(field, start.T)
    return (core, basis.T)


def solution(mesh):
    placed = (P(None, "blk", "grp", None), P())
    return jax.shard_map(
        functools.partial(local, mesh.shape["grp"], mesh.shape["blk"]),
        mesh=mesh,
        in_specs=placed,
        out_specs=(P("grp", "blk", None, None), P()),
        check_vma=False,
    )
```

```python
import functools

import jax
import jax.numpy as jnp
from jax import lax
from jax.experimental import pallas as pl
from jax.experimental.pallas import tpu as pltpu
from jax.sharding import PartitionSpec as P

ITERS = 3
MESH = pl.DeviceIdType.MESH
HIGHEST = lax.Precision.HIGHEST
ANY = pl.BlockSpec(memory_space=pl.ANY)
VMEM = pl.BlockSpec(memory_space=pltpu.VMEM)
NX = 4
NC = 2
ZL = 4


def place(k):
    return k // (NX * NC), (k // NC) % NX, k % NC


def shifted(k, step, ny):
    y, x, core = place(k)
    dy, dx, dcore = place(step)
    return (((y + dy) % ny) * NX + (x + dx) % NX) * NC + (core + dcore) % NC


def wait_bytes(ref, sem):
    pltpu.make_async_copy(ref, ref, sem).wait()


def take(ref, a):
    blocks, halves, rows, _ = ref.shape
    flat = ref.reshape(blocks * halves * rows, 128)
    return jnp.concatenate(
        [flat[pl.ds(half * rows + a, blocks, stride=halves * rows), :] for half in range(halves)], axis=1
    )


def put(ref, a, value):
    blocks, halves, rows, _ = ref.shape
    flat = ref.reshape(blocks * halves * rows, 128)
    for half in range(halves):
        flat[pl.ds(half * rows + a, blocks, stride=halves * rows), :] = value[:, 128 * half : 128 * half + 128]


def inverse_factor(small, rank):
    lane = lax.broadcasted_iota(jnp.int32, (rank, 128), 1)
    row = lax.broadcasted_iota(jnp.int32, (rank, 128), 0)
    first = row[:8]
    tail = jnp.where(lane < 64, jnp.where(lane == row, 1.0, 0.0), small[:rank])
    done = []
    for b in range(rank // 8):
        below = row[: rank - 8 * b]
        columns = [
            jnp.broadcast_to(tail[:, 64 + 8 * b + s : 64 + 8 * b + s + 1], tail.shape) for s in range(8)
        ]
        pivots = jnp.ones((8, 128), jnp.float32)
        for t in range(8):
            pivot = columns[t][t : t + 1, :]
            pivots = jnp.where(first == t, pivot, pivots)
            factor = jnp.where(below > t, columns[t] * (1.0 / pivot), 0.0)
            for s in range(t + 1, 8):
                columns[s] = columns[s] - factor * columns[s][t : t + 1, :]
            tail = tail - factor * tail[t : t + 1, :]
        done.append(tail[:8] / jnp.sqrt(pivots))
        tail = tail[8:]
    return jnp.where(lane < rank, jnp.concatenate(done, axis=0), 0.0)


def split(value):
    high = value.astype(jnp.bfloat16)
    return high, (value - high.astype(jnp.float32)).astype(jnp.bfloat16)


def product(a, b, contract):
    return lax.dot_general(a, b, (contract, ((), ())), preferred_element_type=jnp.float32)


def exact(a, b, contract):
    return lax.dot_general(a, b, (contract, ((), ())), precision=HIGHEST, preferred_element_type=jnp.float32)


def kernel(
    nz,
    nk,
    count,
    field,
    start,
    out,
    basis_out,
    here,
    ready,
    cols,
    tiles,
    core,
    part,
    cross,
    rows_in,
    mine,
    near_in,
    near_sum,
    far_in,
    total,
    held,
    load_sem,
    cols_send,
    cols_recv,
    send_sem,
    recv_sem,
    core_send,
    core_recv,
):
    g, k = lax.axis_index("grp"), lax.axis_index("blk")
    ny = nk // (NX * NC)
    chunks, rank, na = core.shape[0], core.shape[1], core.shape[2]
    ni = field.shape[1]
    each = rank // nk
    y, x, side = place(k)
    zl, zh = g % ZL, g // ZL
    nh = nz // ZL

    def near(step):
        return zh * ZL + (zl + step) % ZL

    def far(step):
        return ((zh + step) % nh) * ZL + zl

    def other(s):
        step = (s - 1 + side * (nk // 2)) % (nk - 1) + 1
        return shifted(k, (step * 13) % nk, ny)

    pltpu.make_async_copy(field, here, load_sem).start()
    barrier = pltpu.get_barrier_semaphore()

    def greet(z, blk):
        pl.semaphore_signal(barrier, inc=1, device_id=(z, blk), device_id_type=MESH)

    @pl.loop(1, nk)
    def _(s):
        greet(g, other(s))

    @pl.loop(1, ZL)
    def _(s):
        greet(near(s), k)

    @pl.loop(1, nh)
    def _(s):
        greet(far(s), k)

    pl.semaphore_wait(barrier, nk - 1 + ZL - 1 + nh - 1)

    def variable(c, x, side):
        zero = (NX - x) // NX
        up = x + c * (nz // 2 - 2 * x)
        down = nz - up + zero * (1 - 2 * c) * (nz // 4) + zero * c * (nz // 2)
        return (g + up + side * (down - up)) % nz

    def piece(c, dest):
        y, x, side = place(dest)
        return ready.at[variable(c, x, side), y]

    def slot(c):
        return cols.at[c, pl.ds(k * ni, ni)]

    wait_bytes(here, load_sem)

    @pl.loop(0, chunks)
    def _(c):
        for place_x in range(NX):
            for place_side in range(NC):
                v = variable(c, place_x, place_side)
                for place_y in range(ny):
                    for half in range(ready.shape[3]):
                        ready[v, place_y, :, half] = here[
                            v, :, na * place_y : na * place_y + na, 128 * half : 128 * half + 128
                        ]

        pltpu.make_async_copy(piece(c, k), slot(c), cols_recv.at[c]).start()

        @pl.loop(1, nk)
        def _(s):
            dest = other(s)
            pltpu.make_async_remote_copy(
                src_ref=piece(c, dest),
                dst_ref=slot(c),
                send_sem=cols_send.at[c],
                recv_sem=cols_recv.at[c],
                device_id=(g, dest),
                device_id_type=MESH,
            ).start()

    part[...] = jnp.zeros_like(part)
    cross[...] = jnp.zeros_like(cross)

    @pl.loop(0, chunks)
    def _(c):
        wait_bytes(cols.at[c], cols_recv.at[c])

        @pl.loop(0, na)
        def _(a):
            high, low = split(take(cols.at[c], a))
            part[...] += product(high, high, ((1,), (1,))) + product(low, low, ((1,), (1,)))
            cross[...] += product(high, low, ((1,), (1,)))

    part[...] += cross[...] + cross[...].T

    own = pl.ds(pl.multiple_of(k * 8, 8), 8)
    rows_in[k] = part[own, :]

    @pl.loop(1, nk)
    def _(s):
        dest = other(s)
        pltpu.make_async_remote_copy(
            src_ref=part.at[pl.ds(pl.multiple_of(dest * 8, 8), 8)],
            dst_ref=rows_in.at[k],
            send_sem=send_sem.at[0],
            recv_sem=recv_sem.at[0],
            device_id=(g, dest),
            device_id_type=MESH,
        ).start()

    wait_bytes(rows_in.at[pl.ds(0, nk - 1)], recv_sem.at[0])
    mine[...] = jnp.sum(rows_in[...], axis=0)
    near_in[zl] = mine[...]

    @pl.loop(1, ZL)
    def _(s):
        pltpu.make_async_remote_copy(
            src_ref=mine,
            dst_ref=near_in.at[zl],
            send_sem=send_sem.at[1],
            recv_sem=recv_sem.at[1],
            device_id=(near(s), k),
            device_id_type=MESH,
        ).start()

    wait_bytes(near_in.at[pl.ds(0, ZL - 1)], recv_sem.at[1])
    near_sum[...] = jnp.sum(near_in[...], axis=0)
    far_in[zh] = near_sum[...]

    @pl.loop(1, nh)
    def _(s):
        pltpu.make_async_remote_copy(
            src_ref=near_sum,
            dst_ref=far_in.at[zh],
            send_sem=send_sem.at[2],
            recv_sem=recv_sem.at[2],
            device_id=(far(s), k),
            device_id_type=MESH,
        ).start()

    wait_bytes(far_in.at[pl.ds(0, nh - 1)], recv_sem.at[2])
    total[k] = jnp.sum(far_in[...], axis=0) * (1.0 / count)

    @pl.loop(1, nk)
    def _(s):
        pltpu.make_async_remote_copy(
            src_ref=total.at[k],
            dst_ref=total.at[k],
            send_sem=send_sem.at[3],
            recv_sem=recv_sem.at[3],
            device_id=(g, other(s)),
            device_id_type=MESH,
        ).start()

    wait_bytes(total.at[pl.ds(0, nk - 1)], recv_sem.at[3])

    half = start[...].T
    if rank < 64:
        half = jnp.concatenate([half, jnp.zeros((half.shape[0], 64 - rank), jnp.float32)], axis=1)
    held[...] = jnp.concatenate([half, half], axis=1)

    @pl.loop(0, ITERS)
    def _(step):
        held[...] = exact(total[...].reshape(part.shape), held[...], ((1,), (0,)))

        @pl.loop(0, 2)
        def _(again):
            block = held[...]
            factor = inverse_factor(exact(block, block, ((0,), (0,))), rank)
            if rank < 64:
                factor = jnp.concatenate([factor, jnp.zeros((64 - rank, 128), jnp.float32)], axis=0)
            held[...] = exact(block, jnp.concatenate([factor, factor], axis=0), ((1,), (1,)))

    turned = held[...].T[:rank]
    basis_out[...] = turned

    high, low = split(turned)
    both = jnp.concatenate([high, low], axis=0)
    place_out = out.at[0, :, pl.ds(pl.multiple_of((g * ny + y) * na, na), na), :]

    @pl.loop(0, chunks)
    def _(c):
        v = variable(c, x, side)

        @pl.loop(0, na)
        def _(a):
            block_high, block_low = split(take(cols.at[c], a))
            first = product(both, block_high, ((1,), (0,)))
            put(tiles, a, first[:rank] + (first[rank:] + product(high, block_low, ((1,), (0,)))))

        for half in range(tiles.shape[1]):
            core[c, :, :, 128 * half : 128 * half + 128] = tiles[:, half]

        def send(dest):
            pltpu.make_async_remote_copy(
                src_ref=core.at[c, pl.ds(dest * each, each)],
                dst_ref=place_out,
                send_sem=core_send,
                recv_sem=core_recv,
                device_id=(v, dest),
                device_id_type=MESH,
            ).start()

        @pl.loop(1, nk)
        def _(s):
            send(other(s))

        @pl.when(v == g)
        def _():
            pltpu.make_async_copy(core.at[c, pl.ds(k * each, each)], place_out, core_recv).start()

        @pl.when(v != g)
        def _():
            send(k)

    @pl.loop(0, chunks)
    def _(c):
        wait_bytes(cols.at[c, pl.ds(0, (nk - 1) * ni)], cols_send.at[c])

    wait_bytes(rows_in.at[pl.ds(0, nk - 1)], send_sem.at[0])
    wait_bytes(near_in.at[pl.ds(0, ZL - 1)], send_sem.at[1])
    wait_bytes(far_in.at[pl.ds(0, nh - 1)], send_sem.at[2])
    wait_bytes(total.at[pl.ds(0, nk - 1)], send_sem.at[3])

    wait_bytes(out, core_recv)

    @pl.when(x + side == 0)
    def _():
        wait_bytes(core.at[pl.ds(0, chunks - 1)], core_send)
        wait_bytes(core.at[chunks - 1, pl.ds(0, rank - each)], core_send)

    @pl.when(x + side != 0)
    def _():
        wait_bytes(core, core_send)


def local(nz, nk, field, start):
    nv, _, na, nb = field.shape
    n1, rank = start.shape
    chunks = 2
    ny = nk // (NX * NC)
    rows = na // ny
    f32 = jnp.float32
    core, basis = pl.pallas_call(
        functools.partial(kernel, nz, nk, nv * na * nz * nb),
        out_shape=(
            jax.ShapeDtypeStruct((nv // nz, rank // nk, na * nz, nb), f32),
            jax.ShapeDtypeStruct((rank, n1), f32),
        ),
        in_specs=[ANY, VMEM],
        out_specs=(ANY, VMEM),
        scratch_shapes=[
            pltpu.VMEM(field.shape, f32),
            pltpu.VMEM((nv, ny, field.shape[1], nb // 128, rows, 128), f32),
            pltpu.VMEM((chunks, n1, nb // 128, rows, 128), f32),
            pltpu.VMEM((rank, nb // 128, rows, 128), f32),
            pltpu.VMEM((chunks, rank, rows, nb), f32),
            pltpu.VMEM((n1, n1), f32),
            pltpu.VMEM((n1, n1), f32),
            pltpu.VMEM((nk, 8, n1), f32),
            pltpu.VMEM((8, n1), f32),
            pltpu.VMEM((ZL, 8, n1), f32),
            pltpu.VMEM((8, n1), f32),
            pltpu.VMEM((nz // ZL, 8, n1), f32),
            pltpu.VMEM((nk, 8, n1), f32),
            pltpu.VMEM((n1, 128), f32),
            pltpu.SemaphoreType.DMA,
            pltpu.SemaphoreType.DMA((chunks,)),
            pltpu.SemaphoreType.DMA((chunks,)),
            pltpu.SemaphoreType.DMA((4,)),
            pltpu.SemaphoreType.DMA((4,)),
            pltpu.SemaphoreType.DMA,
            pltpu.SemaphoreType.DMA,
        ],
        compiler_params=pltpu.CompilerParams(
            collective_id=0, has_side_effects=True, vmem_limit_bytes=60 * 2**20
        ),
        name="whole_step",
    )(field, start.T)
    return (core, basis.T)


def solution(mesh):
    placed = (P(None, "blk", "grp", None), P())
    return jax.shard_map(
        functools.partial(local, mesh.shape["grp"], mesh.shape["blk"]),
        mesh=mesh,
        in_specs=placed,
        out_specs=(P("grp", "blk", None, None), P()),
        check_vma=False,
    )
```

```python
import functools

import jax
import jax.numpy as jnp
from jax import lax
from jax.experimental import pallas as pl
from jax.experimental.pallas import tpu as pltpu
from jax.sharding import PartitionSpec as P

ITERS = 3
MESH = pl.DeviceIdType.MESH
HIGHEST = lax.Precision.HIGHEST
ANY = pl.BlockSpec(memory_space=pl.ANY)
VMEM = pl.BlockSpec(memory_space=pltpu.VMEM)
NX = 4
NC = 2
ZL = 4
ORDER = (
    ((1, 1), (-1, -1)),
    ((-1, -1), (1, 1)),
    ((1, -1), (-1, 1)),
    ((-1, 1), (1, -1)),
    ((2, 1), (-1, 2)),
    ((2, -1), (1, 2)),
    ((1, 2), (2, -1)),
    ((-1, 2), (2, 1)),
    ((2, 2), (2, 2)),
    ((2, 0), (0, 2)),
    ((0, 2), (2, 0)),
    ((1, 0), (-1, 0)),
    ((0, 1), (0, -1)),
    ((-1, 0), (1, 0)),
    ((0, -1), (0, 1)),
)


def place(k):
    return k // (NX * NC), (k // NC) % NX, k % NC


def shifted(k, step, ny):
    y, x, core = place(k)
    dy, dx, dcore = place(step)
    return (((y + dy) % ny) * NX + (x + dx) % NX) * NC + (core + dcore) % NC


def wait_bytes(ref, sem):
    pltpu.make_async_copy(ref, ref, sem).wait()


def take(ref, a):
    blocks, halves, rows, _ = ref.shape
    flat = ref.reshape(blocks * halves * rows, 128)
    return jnp.concatenate(
        [flat[pl.ds(half * rows + a, blocks, stride=halves * rows), :] for half in range(halves)], axis=1
    )


def put(ref, a, value):
    blocks, halves, rows, _ = ref.shape
    flat = ref.reshape(blocks * halves * rows, 128)
    for half in range(halves):
        flat[pl.ds(half * rows + a, blocks, stride=halves * rows), :] = value[:, 128 * half : 128 * half + 128]


def inverse_factor(small, rank):
    lane = lax.broadcasted_iota(jnp.int32, (rank, 128), 1)
    row = lax.broadcasted_iota(jnp.int32, (rank, 128), 0)
    first = row[:8]
    tail = jnp.where(lane < 64, jnp.where(lane == row, 1.0, 0.0), small[:rank])
    done = []
    for b in range(rank // 8):
        below = row[: rank - 8 * b]
        columns = [
            jnp.broadcast_to(tail[:, 64 + 8 * b + s : 64 + 8 * b + s + 1], tail.shape) for s in range(8)
        ]
        pivots = jnp.ones((8, 128), jnp.float32)
        for t in range(8):
            pivot = columns[t][t : t + 1, :]
            pivots = jnp.where(first == t, pivot, pivots)
            factor = jnp.where(below > t, columns[t] * (1.0 / pivot), 0.0)
            for s in range(t + 1, 8):
                columns[s] = columns[s] - factor * columns[s][t : t + 1, :]
            tail = tail - factor * tail[t : t + 1, :]
        done.append(tail[:8] / jnp.sqrt(pivots))
        tail = tail[8:]
    return jnp.where(lane < rank, jnp.concatenate(done, axis=0), 0.0)


def split(value):
    high = value.astype(jnp.bfloat16)
    return high, (value - high.astype(jnp.float32)).astype(jnp.bfloat16)


def product(a, b, contract):
    return lax.dot_general(a, b, (contract, ((), ())), preferred_element_type=jnp.float32)


def exact(a, b, contract):
    return lax.dot_general(a, b, (contract, ((), ())), precision=HIGHEST, preferred_element_type=jnp.float32)


def kernel(
    nz,
    nk,
    count,
    field,
    start,
    out,
    basis_out,
    here,
    ready,
    cols,
    tiles,
    core,
    part,
    cross,
    rows_in,
    mine,
    near_in,
    near_sum,
    far_in,
    total,
    held,
    load_sem,
    cols_send,
    cols_recv,
    send_sem,
    recv_sem,
    core_send,
    core_recv,
):
    g, k = lax.axis_index("grp"), lax.axis_index("blk")
    ny = nk // (NX * NC)
    chunks, rank, na = core.shape[0], core.shape[1], core.shape[2]
    ni = field.shape[1]
    each = rank // nk
    y, x, side = place(k)
    zl, zh = g % ZL, g // ZL
    nh = nz // ZL

    def near(step):
        return zh * ZL + (zl + step) % ZL

    def far(step):
        return ((zh + step) % nh) * ZL + zl

    def other(s):
        step = (s - 1 + side * (nk // 2)) % (nk - 1) + 1
        return shifted(k, (step * 13) % nk, ny)

    pltpu.make_async_copy(field, here, load_sem).start()
    barrier = pltpu.get_barrier_semaphore()

    def greet(z, blk):
        pl.semaphore_signal(barrier, inc=1, device_id=(z, blk), device_id_type=MESH)

    @pl.loop(1, nk)
    def _(s):
        greet(g, other(s))

    @pl.loop(1, ZL)
    def _(s):
        greet(near(s), k)

    @pl.loop(1, nh)
    def _(s):
        greet(far(s), k)

    pl.semaphore_wait(barrier, nk - 1 + ZL - 1 + nh - 1)

    def variable(c, x, side):
        zero = (NX - x) // NX
        up = x + c * (nz // 2 - 2 * x)
        down = nz - up + zero * (1 - 2 * c) * (nz // 4) + zero * c * (nz // 2)
        return (g + up + side * (down - up)) % nz

    def piece(c, dest):
        y, x, side = place(dest)
        return ready.at[variable(c, x, side), y]

    chips = [
        (
            (y + (ny + dy) + side * (dy1 - dy)) % ny,
            (x + (NX + dx) + side * (dx1 - dx)) % NX,
        )
        for (dx, dy), (dx1, dy1) in ORDER
    ]
    listed = [k + 1 - 2 * side] + [
        (to_y * NX + to_x) * NC + (side + dcore) % NC for dcore in (1, 0) for to_y, to_x in chips
    ]

    def slot(c):
        return cols.at[c, pl.ds(k * ni, ni)]

    wait_bytes(here, load_sem)

    @pl.loop(0, chunks)
    def _(c):
        for place_x in range(NX):
            for place_side in range(NC):
                v = variable(c, place_x, place_side)
                for place_y in range(ny):
                    for half in range(ready.shape[3]):
                        ready[v, place_y, :, half] = here[
                            v, :, na * place_y : na * place_y + na, 128 * half : 128 * half + 128
                        ]

        pltpu.make_async_copy(piece(c, k), slot(c), cols_recv.at[c]).start()

        for dest in listed:
            pltpu.make_async_remote_copy(
                src_ref=piece(c, dest),
                dst_ref=slot(c),
                send_sem=cols_send.at[c],
                recv_sem=cols_recv.at[c],
                device_id=(g, dest),
                device_id_type=MESH,
            ).start()

    part[...] = jnp.zeros_like(part)
    cross[...] = jnp.zeros_like(cross)

    @pl.loop(0, chunks)
    def _(c):
        wait_bytes(cols.at[c], cols_recv.at[c])

        @pl.loop(0, na)
        def _(a):
            high, low = split(take(cols.at[c], a))
            part[...] += product(high, high, ((1,), (1,))) + product(low, low, ((1,), (1,)))
            cross[...] += product(high, low, ((1,), (1,)))

    part[...] += cross[...] + cross[...].T

    own = pl.ds(pl.multiple_of(k * 8, 8), 8)
    rows_in[k] = part[own, :]

    @pl.loop(1, nk)
    def _(s):
        dest = other(s)
        pltpu.make_async_remote_copy(
            src_ref=part.at[pl.ds(pl.multiple_of(dest * 8, 8), 8)],
            dst_ref=rows_in.at[k],
            send_sem=send_sem.at[0],
            recv_sem=recv_sem.at[0],
            device_id=(g, dest),
            device_id_type=MESH,
        ).start()

    wait_bytes(rows_in.at[pl.ds(0, nk - 1)], recv_sem.at[0])
    mine[...] = jnp.sum(rows_in[...], axis=0)
    near_in[zl] = mine[...]

    @pl.loop(1, ZL)
    def _(s):
        pltpu.make_async_remote_copy(
            src_ref=mine,
            dst_ref=near_in.at[zl],
            send_sem=send_sem.at[1],
            recv_sem=recv_sem.at[1],
            device_id=(near(s), k),
            device_id_type=MESH,
        ).start()

    wait_bytes(near_in.at[pl.ds(0, ZL - 1)], recv_sem.at[1])
    near_sum[...] = jnp.sum(near_in[...], axis=0)
    far_in[zh] = near_sum[...]

    @pl.loop(1, nh)
    def _(s):
        pltpu.make_async_remote_copy(
            src_ref=near_sum,
            dst_ref=far_in.at[zh],
            send_sem=send_sem.at[2],
            recv_sem=recv_sem.at[2],
            device_id=(far(s), k),
            device_id_type=MESH,
        ).start()

    wait_bytes(far_in.at[pl.ds(0, nh - 1)], recv_sem.at[2])
    total[k] = jnp.sum(far_in[...], axis=0) * (1.0 / count)

    @pl.loop(1, nk)
    def _(s):
        pltpu.make_async_remote_copy(
            src_ref=total.at[k],
            dst_ref=total.at[k],
            send_sem=send_sem.at[3],
            recv_sem=recv_sem.at[3],
            device_id=(g, other(s)),
            device_id_type=MESH,
        ).start()

    wait_bytes(total.at[pl.ds(0, nk - 1)], recv_sem.at[3])

    half = start[...].T
    if rank < 64:
        half = jnp.concatenate([half, jnp.zeros((half.shape[0], 64 - rank), jnp.float32)], axis=1)
    held[...] = jnp.concatenate([half, half], axis=1)

    @pl.loop(0, ITERS)
    def _(step):
        held[...] = exact(total[...].reshape(part.shape), held[...], ((1,), (0,)))

        @pl.loop(0, 2)
        def _(again):
            block = held[...]
            factor = inverse_factor(exact(block, block, ((0,), (0,))), rank)
            if rank < 64:
                factor = jnp.concatenate([factor, jnp.zeros((64 - rank, 128), jnp.float32)], axis=0)
            held[...] = exact(block, jnp.concatenate([factor, factor], axis=0), ((1,), (1,)))

    turned = held[...].T[:rank]
    basis_out[...] = turned

    high, low = split(turned)
    both = jnp.concatenate([high, low], axis=0)
    place_out = out.at[0, :, pl.ds(pl.multiple_of((g * ny + y) * na, na), na), :]

    @pl.loop(0, chunks)
    def _(c):
        v = variable(c, x, side)

        @pl.loop(0, na)
        def _(a):
            block_high, block_low = split(take(cols.at[c], a))
            first = product(both, block_high, ((1,), (0,)))
            put(tiles, a, first[:rank] + (first[rank:] + product(high, block_low, ((1,), (0,)))))

        for half in range(tiles.shape[1]):
            core[c, :, :, 128 * half : 128 * half + 128] = tiles[:, half]

        def send(dest):
            pltpu.make_async_remote_copy(
                src_ref=core.at[c, pl.ds(dest * each, each)],
                dst_ref=place_out,
                send_sem=core_send,
                recv_sem=core_recv,
                device_id=(v, dest),
                device_id_type=MESH,
            ).start()

        @pl.loop(1, nk)
        def _(s):
            send(other(s))

        @pl.when(v == g)
        def _():
            pltpu.make_async_copy(core.at[c, pl.ds(k * each, each)], place_out, core_recv).start()

        @pl.when(v != g)
        def _():
            send(k)

    @pl.loop(0, chunks)
    def _(c):
        wait_bytes(cols.at[c, pl.ds(0, (nk - 1) * ni)], cols_send.at[c])

    wait_bytes(rows_in.at[pl.ds(0, nk - 1)], send_sem.at[0])
    wait_bytes(near_in.at[pl.ds(0, ZL - 1)], send_sem.at[1])
    wait_bytes(far_in.at[pl.ds(0, nh - 1)], send_sem.at[2])
    wait_bytes(total.at[pl.ds(0, nk - 1)], send_sem.at[3])

    wait_bytes(out, core_recv)

    @pl.when(x + side == 0)
    def _():
        wait_bytes(core.at[pl.ds(0, chunks - 1)], core_send)
        wait_bytes(core.at[chunks - 1, pl.ds(0, rank - each)], core_send)

    @pl.when(x + side != 0)
    def _():
        wait_bytes(core, core_send)


def local(nz, nk, field, start):
    nv, _, na, nb = field.shape
    n1, rank = start.shape
    chunks = 2
    ny = nk // (NX * NC)
    rows = na // ny
    f32 = jnp.float32
    core, basis = pl.pallas_call(
        functools.partial(kernel, nz, nk, nv * na * nz * nb),
        out_shape=(
            jax.ShapeDtypeStruct((nv // nz, rank // nk, na * nz, nb), f32),
            jax.ShapeDtypeStruct((rank, n1), f32),
        ),
        in_specs=[ANY, VMEM],
        out_specs=(ANY, VMEM),
        scratch_shapes=[
            pltpu.VMEM(field.shape, f32),
            pltpu.VMEM((nv, ny, field.shape[1], nb // 128, rows, 128), f32),
            pltpu.VMEM((chunks, n1, nb // 128, rows, 128), f32),
            pltpu.VMEM((rank, nb // 128, rows, 128), f32),
            pltpu.VMEM((chunks, rank, rows, nb), f32),
            pltpu.VMEM((n1, n1), f32),
            pltpu.VMEM((n1, n1), f32),
            pltpu.VMEM((nk, 8, n1), f32),
            pltpu.VMEM((8, n1), f32),
            pltpu.VMEM((ZL, 8, n1), f32),
            pltpu.VMEM((8, n1), f32),
            pltpu.VMEM((nz // ZL, 8, n1), f32),
            pltpu.VMEM((nk, 8, n1), f32),
            pltpu.VMEM((n1, 128), f32),
            pltpu.SemaphoreType.DMA,
            pltpu.SemaphoreType.DMA((chunks,)),
            pltpu.SemaphoreType.DMA((chunks,)),
            pltpu.SemaphoreType.DMA((4,)),
            pltpu.SemaphoreType.DMA((4,)),
            pltpu.SemaphoreType.DMA,
            pltpu.SemaphoreType.DMA,
        ],
        compiler_params=pltpu.CompilerParams(
            collective_id=0, has_side_effects=True, vmem_limit_bytes=60 * 2**20
        ),
        name="whole_step",
    )(field, start.T)
    return (core, basis.T)


def solution(mesh):
    placed = (P(None, "blk", "grp", None), P())
    return jax.shard_map(
        functools.partial(local, mesh.shape["grp"], mesh.shape["blk"]),
        mesh=mesh,
        in_specs=placed,
        out_specs=(P("grp", "blk", None, None), P()),
        check_vma=False,
    )
```

```python
import functools

import jax
import jax.numpy as jnp
from jax import lax
from jax.experimental import pallas as pl
from jax.experimental.pallas import tpu as pltpu
from jax.sharding import PartitionSpec as P

ITERS = 3
MESH = pl.DeviceIdType.MESH
HIGHEST = lax.Precision.HIGHEST
ANY = pl.BlockSpec(memory_space=pl.ANY)
VMEM = pl.BlockSpec(memory_space=pltpu.VMEM)
NX = 4
NC = 2
ZL = 4
ORDER = (
    ((1, 1), (-1, -1)),
    ((-1, -1), (1, 1)),
    ((1, -1), (-1, 1)),
    ((-1, 1), (1, -1)),
    ((2, 1), (-1, 2)),
    ((2, -1), (1, 2)),
    ((1, 2), (2, -1)),
    ((-1, 2), (2, 1)),
    ((2, 2), (2, 2)),
    ((2, 0), (0, 2)),
    ((0, 2), (2, 0)),
    ((1, 0), (-1, 0)),
    ((0, 1), (0, -1)),
    ((-1, 0), (1, 0)),
    ((0, -1), (0, 1)),
)


def place(k):
    return k // (NX * NC), (k // NC) % NX, k % NC


def wait_bytes(ref, sem):
    pltpu.make_async_copy(ref, ref, sem).wait()


def take(ref, a):
    blocks, halves, rows, _ = ref.shape
    flat = ref.reshape(blocks * halves * rows, 128)
    return jnp.concatenate(
        [flat[pl.ds(half * rows + a, blocks, stride=halves * rows), :] for half in range(halves)], axis=1
    )


def put(ref, a, value):
    blocks, halves, rows, _ = ref.shape
    flat = ref.reshape(blocks * halves * rows, 128)
    for half in range(halves):
        flat[pl.ds(half * rows + a, blocks, stride=halves * rows), :] = value[:, 128 * half : 128 * half + 128]


def inverse_factor(small, rank):
    lane = lax.broadcasted_iota(jnp.int32, (rank, 128), 1)
    row = lax.broadcasted_iota(jnp.int32, (rank, 128), 0)
    first = row[:8]
    tail = jnp.where(lane < 64, jnp.where(lane == row, 1.0, 0.0), small[:rank])
    done = []
    for b in range(rank // 8):
        below = row[: rank - 8 * b]
        columns = [
            jnp.broadcast_to(tail[:, 64 + 8 * b + s : 64 + 8 * b + s + 1], tail.shape) for s in range(8)
        ]
        pivots = jnp.ones((8, 128), jnp.float32)
        for t in range(8):
            pivot = columns[t][t : t + 1, :]
            pivots = jnp.where(first == t, pivot, pivots)
            factor = jnp.where(below > t, columns[t] * (1.0 / pivot), 0.0)
            for s in range(t + 1, 8):
                columns[s] = columns[s] - factor * columns[s][t : t + 1, :]
            tail = tail - factor * tail[t : t + 1, :]
        done.append(tail[:8] / jnp.sqrt(pivots))
        tail = tail[8:]
    return jnp.where(lane < rank, jnp.concatenate(done, axis=0), 0.0)


def split(value):
    high = value.astype(jnp.bfloat16)
    return high, (value - high.astype(jnp.float32)).astype(jnp.bfloat16)


def product(a, b, contract):
    return lax.dot_general(a, b, (contract, ((), ())), preferred_element_type=jnp.float32)


def exact(a, b, contract):
    return lax.dot_general(a, b, (contract, ((), ())), precision=HIGHEST, preferred_element_type=jnp.float32)


def kernel(
    nz,
    nk,
    count,
    field,
    start,
    out,
    basis_out,
    here,
    ready,
    cols,
    tiles,
    core,
    part,
    cross,
    rows_in,
    mine,
    near_in,
    near_sum,
    far_in,
    total,
    held,
    load_sem,
    cols_send,
    cols_recv,
    send_sem,
    recv_sem,
    core_send,
    core_recv,
):
    g, k = lax.axis_index("grp"), lax.axis_index("blk")
    ny = nk // (NX * NC)
    chunks, rank, na = core.shape[0], core.shape[1], core.shape[2]
    ni = field.shape[1]
    each = rank // nk
    y, x, side = place(k)
    zl, zh = g % ZL, g // ZL
    nh = nz // ZL

    def near(step):
        return zh * ZL + (zl + step) % ZL

    def far(step):
        return ((zh + step) % nh) * ZL + zl

    pltpu.make_async_copy(field, here, load_sem).start()
    barrier = pltpu.get_barrier_semaphore()

    def greet(z, blk):
        pl.semaphore_signal(barrier, inc=1, device_id=(z, blk), device_id_type=MESH)

    @pl.loop(1, nk)
    def _(s):
        greet(g, (k + s) % nk)

    @pl.loop(1, ZL)
    def _(s):
        greet(near(s), k)

    @pl.loop(1, nh)
    def _(s):
        greet(far(s), k)

    pl.semaphore_wait(barrier, nk - 1 + ZL - 1 + nh - 1)

    def variable(c, x, side):
        zero = (NX - x) // NX
        up = x + c * (nz // 2 - 2 * x)
        down = nz - up + zero * (1 - 2 * c) * (nz // 4) + zero * c * (nz // 2)
        return (g + up + side * (down - up)) % nz

    def piece(c, dest):
        y, x, side = place(dest)
        return ready.at[variable(c, x, side), y]

    chips = [
        (
            (y + (ny + dy) + side * (dy1 - dy)) % ny,
            (x + (NX + dx) + side * (dx1 - dx)) % NX,
        )
        for (dx, dy), (dx1, dy1) in ORDER
    ]
    listed = [k + 1 - 2 * side] + [
        (to_y * NX + to_x) * NC + (side + dcore) % NC for dcore in (1, 0) for to_y, to_x in chips
    ]

    def slot(c):
        return cols.at[c, pl.ds(k * ni, ni)]

    wait_bytes(here, load_sem)

    @pl.loop(0, chunks)
    def _(c):
        for place_x in range(NX):
            for place_side in range(NC):
                v = variable(c, place_x, place_side)
                for place_y in range(ny):
                    for half in range(ready.shape[3]):
                        ready[v, place_y, :, half] = here[
                            v, :, na * place_y : na * place_y + na, 128 * half : 128 * half + 128
                        ]

        pltpu.make_async_copy(piece(c, k), slot(c), cols_recv.at[c]).start()

        for dest in listed:
            pltpu.make_async_remote_copy(
                src_ref=piece(c, dest),
                dst_ref=slot(c),
                send_sem=cols_send.at[c],
                recv_sem=cols_recv.at[c],
                device_id=(g, dest),
                device_id_type=MESH,
            ).start()

    part[...] = jnp.zeros_like(part)
    cross[...] = jnp.zeros_like(cross)

    @pl.loop(0, chunks)
    def _(c):
        wait_bytes(cols.at[c], cols_recv.at[c])

        @pl.loop(0, na, unroll=4)
        def _(a):
            high, low = split(take(cols.at[c], a))
            part[...] += product(high, high, ((1,), (1,))) + product(low, low, ((1,), (1,)))
            cross[...] += product(high, low, ((1,), (1,)))

    part[...] += cross[...] + cross[...].T

    own = pl.ds(pl.multiple_of(k * 8, 8), 8)
    rows_in[k] = part[own, :]

    for dest in listed:
        pltpu.make_async_remote_copy(
            src_ref=part.at[pl.ds(pl.multiple_of(dest * 8, 8), 8)],
            dst_ref=rows_in.at[k],
            send_sem=send_sem.at[0],
            recv_sem=recv_sem.at[0],
            device_id=(g, dest),
            device_id_type=MESH,
        ).start()

    wait_bytes(rows_in.at[pl.ds(0, nk - 1)], recv_sem.at[0])
    mine[...] = jnp.sum(rows_in[...], axis=0)
    near_in[zl] = mine[...]

    @pl.loop(1, ZL)
    def _(s):
        pltpu.make_async_remote_copy(
            src_ref=mine,
            dst_ref=near_in.at[zl],
            send_sem=send_sem.at[1],
            recv_sem=recv_sem.at[1],
            device_id=(near(s), k),
            device_id_type=MESH,
        ).start()

    wait_bytes(near_in.at[pl.ds(0, ZL - 1)], recv_sem.at[1])
    near_sum[...] = jnp.sum(near_in[...], axis=0)
    far_in[zh] = near_sum[...]

    @pl.loop(1, nh)
    def _(s):
        pltpu.make_async_remote_copy(
            src_ref=near_sum,
            dst_ref=far_in.at[zh],
            send_sem=send_sem.at[2],
            recv_sem=recv_sem.at[2],
            device_id=(far(s), k),
            device_id_type=MESH,
        ).start()

    wait_bytes(far_in.at[pl.ds(0, nh - 1)], recv_sem.at[2])
    total[k] = jnp.sum(far_in[...], axis=0) * (1.0 / count)

    for dest in listed:
        pltpu.make_async_remote_copy(
            src_ref=total.at[k],
            dst_ref=total.at[k],
            send_sem=send_sem.at[3],
            recv_sem=recv_sem.at[3],
            device_id=(g, dest),
            device_id_type=MESH,
        ).start()

    wait_bytes(total.at[pl.ds(0, nk - 1)], recv_sem.at[3])

    half = start[...].T
    if rank < 64:
        half = jnp.concatenate([half, jnp.zeros((half.shape[0], 64 - rank), jnp.float32)], axis=1)
    held[...] = jnp.concatenate([half, half], axis=1)

    @pl.loop(0, ITERS)
    def _(step):
        held[...] = exact(total[...].reshape(part.shape), held[...], ((1,), (0,)))

        @pl.loop(0, 2)
        def _(again):
            block = held[...]
            factor = inverse_factor(exact(block, block, ((0,), (0,))), rank)
            if rank < 64:
                factor = jnp.concatenate([factor, jnp.zeros((64 - rank, 128), jnp.float32)], axis=0)
            held[...] = exact(block, jnp.concatenate([factor, factor], axis=0), ((1,), (1,)))

    turned = held[...].T[:rank]
    basis_out[...] = turned

    high, low = split(turned)
    both = jnp.concatenate([high, low], axis=0)
    place_out = out.at[0, :, pl.ds(pl.multiple_of((g * ny + y) * na, na), na), :]

    @pl.loop(0, chunks)
    def _(c):
        v = variable(c, x, side)

        @pl.loop(0, na, unroll=4)
        def _(a):
            block_high, block_low = split(take(cols.at[c], a))
            first = product(both, block_high, ((1,), (0,)))
            put(tiles, a, first[:rank] + (first[rank:] + product(high, block_low, ((1,), (0,)))))

        for half in range(tiles.shape[1]):
            core[c, :, :, 128 * half : 128 * half + 128] = tiles[:, half]

        def send(dest):
            pltpu.make_async_remote_copy(
                src_ref=core.at[c, pl.ds(dest * each, each)],
                dst_ref=place_out,
                send_sem=core_send,
                recv_sem=core_recv,
                device_id=(v, dest),
                device_id_type=MESH,
            ).start()

        for dest in listed:
            send(dest)

        @pl.when(v == g)
        def _():
            pltpu.make_async_copy(core.at[c, pl.ds(k * each, each)], place_out, core_recv).start()

        @pl.when(v != g)
        def _():
            send(k)

    @pl.loop(0, chunks)
    def _(c):
        wait_bytes(cols.at[c, pl.ds(0, (nk - 1) * ni)], cols_send.at[c])

    wait_bytes(rows_in.at[pl.ds(0, nk - 1)], send_sem.at[0])
    wait_bytes(near_in.at[pl.ds(0, ZL - 1)], send_sem.at[1])
    wait_bytes(far_in.at[pl.ds(0, nh - 1)], send_sem.at[2])
    wait_bytes(total.at[pl.ds(0, nk - 1)], send_sem.at[3])

    wait_bytes(out, core_recv)

    @pl.when(x + side == 0)
    def _():
        wait_bytes(core.at[pl.ds(0, chunks - 1)], core_send)
        wait_bytes(core.at[chunks - 1, pl.ds(0, rank - each)], core_send)

    @pl.when(x + side != 0)
    def _():
        wait_bytes(core, core_send)


def local(nz, nk, field, start):
    nv, _, na, nb = field.shape
    n1, rank = start.shape
    chunks = 2
    ny = nk // (NX * NC)
    rows = na // ny
    f32 = jnp.float32
    core, basis = pl.pallas_call(
        functools.partial(kernel, nz, nk, nv * na * nz * nb),
        out_shape=(
            jax.ShapeDtypeStruct((nv // nz, rank // nk, na * nz, nb), f32),
            jax.ShapeDtypeStruct((rank, n1), f32),
        ),
        in_specs=[ANY, VMEM],
        out_specs=(ANY, VMEM),
        scratch_shapes=[
            pltpu.VMEM(field.shape, f32),
            pltpu.VMEM((nv, ny, field.shape[1], nb // 128, rows, 128), f32),
            pltpu.VMEM((chunks, n1, nb // 128, rows, 128), f32),
            pltpu.VMEM((rank, nb // 128, rows, 128), f32),
            pltpu.VMEM((chunks, rank, rows, nb), f32),
            pltpu.VMEM((n1, n1), f32),
            pltpu.VMEM((n1, n1), f32),
            pltpu.VMEM((nk, 8, n1), f32),
            pltpu.VMEM((8, n1), f32),
            pltpu.VMEM((ZL, 8, n1), f32),
            pltpu.VMEM((8, n1), f32),
            pltpu.VMEM((nz // ZL, 8, n1), f32),
            pltpu.VMEM((nk, 8, n1), f32),
            pltpu.VMEM((n1, 128), f32),
            pltpu.SemaphoreType.DMA,
            pltpu.SemaphoreType.DMA((chunks,)),
            pltpu.SemaphoreType.DMA((chunks,)),
            pltpu.SemaphoreType.DMA((4,)),
            pltpu.SemaphoreType.DMA((4,)),
            pltpu.SemaphoreType.DMA,
            pltpu.SemaphoreType.DMA,
        ],
        compiler_params=pltpu.CompilerParams(
            collective_id=0, has_side_effects=True, vmem_limit_bytes=50 * 2**20
        ),
        name="whole_step",
    )(field, start.T)
    return (core, basis.T)


def solution(mesh):
    placed = (P(None, "blk", "grp", None), P())
    return jax.shard_map(
        functools.partial(local, mesh.shape["grp"], mesh.shape["blk"]),
        mesh=mesh,
        in_specs=placed,
        out_specs=(P("grp", "blk", None, None), P()),
        check_vma=False,
    )
```
